32 devices in a mesh: rows: 8 (over z, x), cols: 4 (over y, core).
Axes of the slice: x: 2, y: 2, z: 4, core: 2. Of those that a mesh axis runs over, the one named last changes fastest.
Arguments:
- ham_tiles: bfloat16 [32, 8, 256, 256], P('rows', 'cols'), may hold values from -0.0625 to 0.0625
- tile_cols: int32 [32, 8], P('rows'), may hold values from -4 to 35, as said below
- tile_count: int32 [32], P('rows'), may hold values from 1 to 8
- term_prev: bfloat16 [8192, 1024], P('rows', 'cols'), may hold values from -0.29882812 to 0.29882812
- term_now: bfloat16 [8192, 1024], P('rows', 'cols'), may hold values from -0.29882812 to 0.29882812
- density_prev: float32 [8192, 1024], P('rows', 'cols'), may hold values from -0.3 to 0.3
- cheb_coef: float32 [3], replicated, may hold values from -1.5 to 1.5
- atom_sizes: int32 [1024], replicated, may hold values from 1 to 16, 8192 in all
- pair_atoms: int32 [64, 2], P('cols'), may hold values from 0 to 1023
Outputs:
- density: float32 [8192, 1024], P('rows', 'cols')
- wiberg: float32 [64], P('cols')
The draws below stay inside these ranges and needn't reach their ends.
Inputs may be any that keep to these rules, and one draw needn't show every extreme that they name: tile_cols[i, 0] = i; the other slots of row i are distinct column tiles within 4 of i, possibly outside 0 to 32 - 1 (then not live).
All inputs are finite; a program needn't handle non-finite values.
Results may differ from the reference program's by a relative error of at most 0.006.
Values may be sent and summed in bfloat16 or wider, within the bound.
A program may use at most 64 MiB of HBM per device.

```python
import math
import jax
import jax.numpy as jnp
import numpy as np
from jax import lax

B = 256
R = 4
K = 8
MAXF = 16
NPAIRS = 64
NB = 32
NBAS = 8192
NATOMS = 1024
W = 1024
N_ROWS = 8


def draw_tile_cols(key, part):
    span = 2 * R
    scores = jax.random.randint(key, (NB, span), 0, 1 << 20) * span + jnp.arange(span, dtype=jnp.int32)[None, :]
    order = jnp.argsort(scores, axis=1)
    candidates = jnp.concatenate([jnp.arange(R, dtype=jnp.int32) - R, jnp.arange(R, dtype=jnp.int32) + 1])
    picks = candidates[order[:, :K - 1]]
    shifts = jnp.concatenate([jnp.zeros((NB, 1), jnp.int32), picks], axis=1)
    return (jnp.arange(NB, dtype=jnp.int32)[:, None] + shifts).astype(jnp.int32)


def plant(array, own_key, least, top_value):
    longest = array.shape.index(max(array.shape))
    spots = []
    for shift in (0, 1):
        where = [jax.random.randint(jax.random.fold_in(own_key, axis), (), 0, length) for axis, length in enumerate(array.shape)]
        where[longest] = (where[longest] + shift) % array.shape[longest]
        spots.append(tuple(where))
    return array.at[spots[0]].set(least).at[spots[1]].set(top_value)


def levels(stream_key, shape, shards, low, largest):
    def one(dim, shards_of):
        draws = jax.random.uniform(jax.random.fold_in(jax.random.fold_in(stream_key, 6), dim), (shards_of,), jnp.float32, low / len(shards), largest / len(shards))
        return jnp.repeat(jnp.exp(draws), shape[dim] // shards_of).reshape((-1,) + (1,) * (len(shape) - dim - 1))

    factor_of = one(*shards[0])
    for cut in shards[1:]:
        factor_of = factor_of * one(*cut)
    return factor_of


def length_profile(number_of, total, bound, slope):
    weights = [(1 << 20) // math.isqrt(rank ** slope) + 1 for rank in range(2, number_of + 1)]
    spare, given = total - bound - (number_of - 1), [1] * (number_of - 1)
    while spare > 0:
        free = [i for i in range(number_of - 1) if given[i] < bound]
        mass, budget = sum([weights[i] for i in free]), spare
        for i in free:
            addition = min(bound - given[i], max(1, budget * weights[i] // mass), spare)
            given[i] = given[i] + addition
            spare = spare - addition
    return np.array([bound] + given)


def ragged_sizes(stream_key, count, total, limit, skew):
    if count == 2:
        one = jax.random.randint(stream_key, (), max(1, total - limit), min(limit, total - 1) + 1)
        return jnp.stack([one, total - one])
    lengths = jnp.asarray(length_profile(count, total, limit, skew), jnp.int32)
    twos = (count - 1) // 2
    donor, sink = lengths[1:1 + 2 * twos:2], lengths[2:2 + 2 * twos:2]
    room = jnp.minimum(donor - 1, limit - sink)
    shifted = jax.random.randint(jax.random.fold_in(stream_key, 1), (twos,), 0, 1 << 20) % (room + 1)
    lengths = lengths.at[1:1 + 2 * twos:2].set(donor - shifted).at[2:2 + 2 * twos:2].set(sink + shifted)
    return lengths[jax.random.permutation(jax.random.fold_in(stream_key, 2), count)]


def normal_values(key, dims, scale, limit, split=(), kind=jnp.bfloat16):
    result = scale * jax.random.normal(key, dims, jnp.float32)
    if split:
        result = result * levels(key, dims, split, -0.22, 0.18)
    return jnp.clip(result, -limit, limit).astype(kind)


def setup_inputs(seed: int = 0) -> dict:
    keys = jax.random.split(jax.random.key(seed), 10)
    ham_tiles = normal_values(keys[0], (NB, K, B, B), (4 * K * B) ** -0.5, 0.0625, ((0, 8), (1, 4)))
    tile_cols = draw_tile_cols(jax.random.fold_in(keys[9], 71), 0)
    tile_count = plant(jax.random.randint(keys[2], (NB,), 1, K + 1), jax.random.fold_in(keys[2], 1), 1, K).astype(jnp.int32)
    term_prev = normal_values(keys[3], (NBAS, W), 0.05, 0.29882812, ((0, 8), (1, 4)))
    term_now = normal_values(keys[4], (NBAS, W), 0.05, 0.29882812, ((0, 8), (1, 4)))
    density_prev = normal_values(keys[5], (NBAS, W), 0.05, 0.3, ((0, 8), (1, 4)), jnp.float32)
    cheb_coef = jnp.clip(jax.random.uniform(keys[6], (3,), jnp.float32, -1.5, 1.5), -1.5, 1.5)
    atom_sizes = ragged_sizes(keys[7], NATOMS, NBAS, MAXF, 0).astype(jnp.int32)
    pair_atoms = plant(jax.random.randint(keys[8], (NPAIRS, 2), 0, NATOMS), jax.random.fold_in(keys[8], 1), 0, NATOMS - 1).astype(jnp.int32)
    return dict(ham_tiles=ham_tiles, tile_cols=tile_cols, tile_count=tile_count, term_prev=term_prev, term_now=term_now, density_prev=density_prev, cheb_coef=cheb_coef, atom_sizes=atom_sizes, pair_atoms=pair_atoms)


def reference(ham_tiles, tile_cols, tile_count, term_prev, term_now, density_prev, cheb_coef, atom_sizes, pair_atoms):
    nblk = R * N_ROWS
    width = NPAIRS * MAXF
    slots = jnp.arange(K, dtype=jnp.int32)
    live = (slots[None, :] < tile_count[:, None]) & (tile_cols >= 0) & (tile_cols < nblk)
    safe = jnp.clip(tile_cols, 0, nblk - 1).astype(jnp.int32)
    masked = ham_tiles * live[:, :, None, None].astype(jnp.bfloat16)

    def apply(vec):
        tiles = vec.reshape(nblk, B, width)

        def single(args):
            block, columns = args
            chosen = tiles[columns]
            return jnp.einsum("kab,kbw->aw", block.astype(jnp.float32), chosen.astype(jnp.float32))

        return lax.map(single, (masked, safe)).reshape(nblk * B, width)

    previous, current = term_prev, term_now
    density = density_prev
    for step in range(3):
        nxt = (2.0 * apply(current) - previous.astype(jnp.float32)).astype(jnp.bfloat16)
        density = density + cheb_coef[step] * nxt.astype(jnp.float32)
        previous, current = current, nxt
    offsets = (jnp.cumsum(atom_sizes) - atom_sizes).astype(jnp.int32)
    first = pair_atoms[:, 0]
    second = pair_atoms[:, 1]
    start = offsets[first]
    count_a = atom_sizes[first]
    count_b = atom_sizes[second]
    inner = jnp.arange(MAXF, dtype=jnp.int32)
    rowsel = jnp.clip(start[:, None] + inner[None, :], 0, nblk * B - 1).astype(jnp.int32)
    grouped = density.reshape(nblk * B, NPAIRS, MAXF)
    blocks = grouped[rowsel, jnp.arange(NPAIRS, dtype=jnp.int32)[:, None]]
    keep = (inner[None, :, None] < count_a[:, None, None]) & (inner[None, None, :] < count_b[:, None, None])
    wiberg = jnp.sum(jnp.where(keep, blocks * blocks, 0.0), axis=(1, 2))
    return density, wiberg
```

```python
import functools

import jax
import jax.numpy as jnp
from jax import lax
from jax.experimental import pallas as pl
from jax.experimental.pallas import tpu as pltpu
from jax.sharding import PartitionSpec as P

MAXF = 16
STEPS = 3
CHUNKS = 2
MESH = pl.DeviceIdType.MESH


def kernel(
    n,
    ham,
    cols_ref,
    count_ref,
    prev_ref,
    now_ref,
    dens_in,
    coef,
    sizes,
    pairs,
    dens,
    wib,
    hb,
    part,
    wbuf,
    h_send,
    h_recv,
    t_send,
    t_recv,
    w_send,
    w_recv,
    *bufs,
):
    ext = [bufs[t * CHUNKS : (t + 1) * CHUNKS] for t in range(STEPS)]
    me = lax.axis_index("rows")
    mc = lax.axis_index("cols")
    blocks, own_slots, tile, _ = ham.shape
    width = now_ref.shape[1] // CHUNKS
    zero_tile = 3 * blocks
    sib = mc + 1 - 2 * (mc % 2)
    far = (mc + 2) % 4

    barrier = pltpu.get_barrier_semaphore()

    def greet(j, carry):
        pl.semaphore_signal(barrier, inc=1, device_id={"rows": (me + j) % n}, device_id_type=MESH)
        return carry

    lax.fori_loop(1, n, greet, 0)
    pl.semaphore_signal(barrier, inc=1, device_id={"cols": sib}, device_id_type=MESH)
    pl.semaphore_signal(barrier, inc=1, device_id={"cols": far}, device_id_type=MESH)

    def put(t, ch, l, value):
        ext[t][ch][blocks + l] = value

    for ch in range(CHUNKS):
        for l in range(blocks):
            put(0, ch, l, now_ref[l * tile : (l + 1) * tile, ch * width : (ch + 1) * width])
    for t in range(STEPS):
        for ch in range(CHUNKS):
            ext[t][ch][zero_tile] = jnp.zeros((tile, width), jnp.bfloat16)
    pl.semaphore_wait(barrier, n + 1)

    def halo(t, ch, up):
        return pltpu.make_async_remote_copy(
            src_ref=ext[t][ch].at[pl.ds(blocks, blocks)],
            dst_ref=ext[t][ch].at[pl.ds(0 if up else 2 * blocks, blocks)],
            send_sem=t_send.at[t, ch, int(up)],
            recv_sem=t_recv.at[t, ch, int(up)],
            device_id={"rows": me + 1 if up else me - 1},
            device_id_type=MESH,
        )

    def send_halo(t, ch):
        @pl.when(me < n - 1)
        def _():
            halo(t, ch, True).start()

        @pl.when(me > 0)
        def _():
            halo(t, ch, False).start()

    def recv_halo(t, ch):
        @pl.when(me > 0)
        def _():
            halo(t, ch, True).wait_recv()

        @pl.when(me < n - 1)
        def _():
            halo(t, ch, False).wait_recv()

    def drain_halo(t, ch):
        @pl.when(me < n - 1)
        def _():
            halo(t, ch, True).wait_send()

        @pl.when(me > 0)
        def _():
            halo(t, ch, False).wait_send()

    def tiles(q, l):
        return pltpu.make_async_remote_copy(
            src_ref=hb.at[1, l] if q == 2 else ham.at[l],
            dst_ref=hb.at[q, l],
            send_sem=h_send.at[q, l],
            recv_sem=h_recv.at[q, l],
            device_id={"cols": far if q == 1 else sib},
            device_id_type=MESH,
        )

    for ch in range(CHUNKS):
        send_halo(0, ch)
        for l in range(blocks):
            if l % CHUNKS == ch:
                tiles(1, l).start()
    for l in range(blocks):
        tiles(0, l).start()

    dens[...] = dens_in[...]

    npairs = pairs.shape[0]
    natoms = sizes.shape[1]
    atom = lax.broadcasted_iota(jnp.int32, (npairs, natoms), 1)
    size_f = jnp.broadcast_to(sizes[...].astype(jnp.float32), (npairs, natoms))
    first = jnp.broadcast_to(pairs[:, 0:1], (npairs, natoms))
    second = jnp.broadcast_to(pairs[:, 1:2], (npairs, natoms))
    start = jnp.sum(jnp.where(atom < first, size_f, 0.0), axis=1, keepdims=True)
    count_a = jnp.sum(jnp.where(atom == first, size_f, 0.0), axis=1, keepdims=True)
    count_b = jnp.sum(jnp.where(atom == second, size_f, 0.0), axis=1, keepdims=True)
    all_cols = npairs * MAXF
    column = lax.broadcasted_iota(jnp.int32, (npairs, all_cols), 1)
    pair_id = lax.broadcasted_iota(jnp.int32, (npairs, all_cols), 0)
    inner = column - pair_id * MAXF
    mine = (inner >= 0) & (inner < MAXF)
    kept = mine & (inner.astype(jnp.float32) < jnp.broadcast_to(count_b, (npairs, all_cols)))

    def spread(value, where):
        return jnp.sum(
            jnp.where(where, jnp.broadcast_to(value, (npairs, all_cols)), 0.0), axis=0, keepdims=True
        )

    low = spread(start, mine)
    high = low + spread(count_a, kept)
    part[...] = jnp.zeros_like(part)

    for l in range(blocks):
        tiles(1, l).wait_recv()
        tiles(2, l).start()
    for q in (0, 2):
        for l in range(blocks):
            tiles(q, l).wait_recv()

    owners = (mc, sib, far, (sib + 2) % 4)
    base = me * blocks

    def where_is(l, slot):
        col = cols_ref[l, slot]
        live = (slot < count_ref[l]) & (col >= 0) & (col < blocks * n)
        return jnp.where(live, jnp.clip(col - base + blocks, 0, 3 * blocks - 1), zero_tile)

    for t in range(STEPS):
        for ch in range(CHUNKS):
            span = slice(ch * width, (ch + 1) * width)
            recv_halo(t, ch)

            def row(l, carry, t=t, ch=ch, span=span):
                acc = jnp.zeros((tile, width), jnp.float32)
                for q, owner in enumerate(owners):
                    for s in range(own_slots):
                        h = ham[l, s] if q == 0 else hb[q - 1, l, s]
                        v = ext[t][ch][where_is(l, owner * own_slots + s)]
                        acc += jnp.dot(h, v, preferred_element_type=jnp.float32)
                rows = pl.ds(pl.multiple_of(l * tile, tile), tile)
                if t == 0:
                    prev = prev_ref[rows, span]
                else:
                    prev = ext[t - 1][ch][blocks + l]
                nxt = (2.0 * acc - prev.astype(jnp.float32)).astype(jnp.bfloat16)
                value = dens[rows, span] + coef[t] * nxt.astype(jnp.float32)
                dens[rows, span] = value
                if t < STEPS - 1:
                    ext[t + 1][ch][blocks + l] = nxt
                else:
                    r = lax.broadcasted_iota(jnp.int32, (tile, width), 0) + (base + l) * tile
                    r = r.astype(jnp.float32)
                    keep = (r >= low[:, span]) & (r < high[:, span])
                    sq = jnp.where(keep, value * value, 0.0)
                    part[:, span] += jnp.sum(sq.reshape(tile // 8, 8, width), axis=0)
                return carry

            lax.fori_loop(0, blocks, row, 0)
            if t < STEPS - 1:
                send_halo(t + 1, ch)

    def share(j):
        return pltpu.make_async_remote_copy(
            src_ref=part,
            dst_ref=wbuf.at[me],
            send_sem=w_send.at[j],
            recv_sem=w_recv.at[me],
            device_id={"rows": (me + j) % n},
            device_id_type=MESH,
        )

    def landed(j):
        source = (me + j) % n
        return pltpu.make_async_remote_copy(
            src_ref=part,
            dst_ref=wbuf.at[source],
            send_sem=w_send.at[j],
            recv_sem=w_recv.at[source],
            device_id={"rows": source},
            device_id_type=MESH,
        )

    def push(j, carry):
        share(j).start()
        return carry

    lax.fori_loop(1, n, push, 0)
    for l in range(blocks):
        for q in range(3):
            tiles(q, l).wait_send()
    for t in range(STEPS):
        for ch in range(CHUNKS):
            drain_halo(t, ch)

    def collect(j, total):
        landed(j).wait_recv()
        return total + wbuf[(me + j) % n]

    total = lax.fori_loop(1, n, collect, part[...])
    summed = jnp.broadcast_to(jnp.sum(total, axis=0, keepdims=True), (npairs, all_cols))
    wib[...] = jnp.sum(jnp.where(mine, summed, 0.0), axis=1, keepdims=True)

    def drain(j, carry):
        share(j).wait_send()
        return carry

    lax.fori_loop(1, n, drain, 0)


def on_device(n, ham, cols, count, prev, now, dens_prev, coef, sizes, pairs):
    blocks, own_slots, tile, _ = ham.shape
    rows, width = now.shape
    npairs = pairs.shape[0]
    vmem = pl.BlockSpec(memory_space=pltpu.VMEM)
    smem = pl.BlockSpec(memory_space=pltpu.SMEM)
    dma = pltpu.SemaphoreType.DMA
    dens, wib = pl.pallas_call(
        functools.partial(kernel, n),
        out_shape=(
            jax.ShapeDtypeStruct((rows, width), jnp.float32),
            jax.ShapeDtypeStruct((npairs, 1), jnp.float32),
        ),
        in_specs=[vmem, smem, smem, vmem, vmem, vmem, smem, vmem, vmem],
        out_specs=(vmem, vmem),
        scratch_shapes=[
            pltpu.VMEM((3, blocks, own_slots, tile, tile), jnp.bfloat16),
            pltpu.VMEM((8, width), jnp.float32),
            pltpu.VMEM((n, 8, width), jnp.float32),
            dma((3, blocks)),
            dma((3, blocks)),
            dma((STEPS, CHUNKS, 2)),
            dma((STEPS, CHUNKS, 2)),
            dma((n,)),
            dma((n,)),
        ]
        + [pltpu.VMEM((3 * blocks + 1, tile, width // CHUNKS), jnp.bfloat16)] * (STEPS * CHUNKS),
        compiler_params=pltpu.CompilerParams(
            collective_id=0, has_side_effects=True, vmem_limit_bytes=48 << 20
        ),
    )(ham, cols, count, prev, now, dens_prev, coef, sizes.reshape(1, -1), pairs)
    return dens, wib.reshape(npairs)


def solution(mesh):
    return jax.shard_map(
        functools.partial(on_device, mesh.shape["rows"]),
        mesh=mesh,
        in_specs=(
            P("rows", "cols", None, None),
            P("rows", None),
            P("rows"),
            P("rows", "cols"),
            P("rows", "cols"),
            P("rows", "cols"),
            P(),
            P(),
            P("cols", None),
        ),
        out_specs=(P("rows", "cols"), P("cols")),
        check_vma=False,
    )
```

```python
import functools

import jax
import jax.numpy as jnp
from jax import lax
from jax.experimental import pallas as pl
from jax.experimental.pallas import tpu as pltpu
from jax.sharding import PartitionSpec as P

MAXF = 16
STEPS = 3
MESH = pl.DeviceIdType.MESH


def kernel(
    n,
    ham,
    cols_ref,
    count_ref,
    prev_ref,
    now_ref,
    dens_in,
    coef,
    sizes,
    pairs,
    dens,
    wib,
    hown,
    hb,
    pv,
    fin,
    vmine,
    vpair,
    smine,
    spair,
    part,
    bounds,
    wbuf,
    h_send,
    h_recv,
    t_send,
    t_recv,
    i_send,
    i_recv,
    r_send,
    r_recv,
    w_send,
    w_recv,
    l_sem,
    *bufs,
):
    ext, ret = bufs[:STEPS], bufs[STEPS:]
    me = lax.axis_index("rows")
    mc = lax.axis_index("cols")
    x = me % 2
    y = 1 - x
    mate = me + 1 - 2 * x
    blocks, own_slots, tile, _ = ham.shape
    half = now_ref.shape[1] // 2
    zero_tile = 4 * blocks
    sib = mc + 1 - 2 * (mc % 2)
    far = (mc + 2) % 4
    here = pl.ds(pl.multiple_of(x * half, half), half)
    there = pl.ds(pl.multiple_of(y * half, half), half)

    def remote(src, dst, send, recv, device):
        return pltpu.make_async_remote_copy(
            src_ref=src, dst_ref=dst, send_sem=send, recv_sem=recv, device_id=device, device_id_type=MESH
        )

    local = [pltpu.make_async_copy(ham, hown, l_sem.at[0]), pltpu.make_async_copy(dens_in, dens, l_sem.at[1])]
    for l in range(blocks):
        rows = pl.ds(l * tile, tile)
        local.append(
            pltpu.make_async_copy(now_ref.at[rows, here], ext[0].at[blocks + x * blocks + l], l_sem.at[2 + 2 * l])
        )
        local.append(pltpu.make_async_copy(prev_ref.at[rows, here], pv.at[x * blocks + l], l_sem.at[3 + 2 * l]))
    for c in local[2:] + local[:2]:
        c.start()

    barrier = pltpu.get_barrier_semaphore()

    def greet(j, carry):
        pl.semaphore_signal(barrier, inc=1, device_id={"rows": (me + j) % n}, device_id_type=MESH)
        return carry

    lax.fori_loop(1, n, greet, 0)
    pl.semaphore_signal(barrier, inc=1, device_id={"cols": sib}, device_id_type=MESH)
    pl.semaphore_signal(barrier, inc=1, device_id={"cols": far}, device_id_type=MESH)

    first_tile = (me - x) * blocks
    nslots = cols_ref.shape[1]
    tc = cols_ref[...]
    slot_id = lax.broadcasted_iota(jnp.int32, (blocks, nslots), 1)
    live = (slot_id < jnp.broadcast_to(count_ref[...], (blocks, nslots))) & (tc >= 0) & (tc < blocks * n)
    place = jnp.where(live, jnp.clip(tc - first_tile + blocks, 0, zero_tile - 1), zero_tile)
    vmine[...] = jnp.full(vmine.shape, zero_tile, jnp.int32)
    vmine[0:blocks, 0:nslots] = place
    for t in range(STEPS):
        ext[t][zero_tile] = jnp.zeros((tile, half), jnp.bfloat16)
    pl.semaphore_wait(barrier, n + 1)

    def start_tile(src, l):
        rows = pl.ds(l * tile, tile)
        if src == 0:
            return remote(
                now_ref.at[rows, there], ext[0].at[blocks + x * blocks + l],
                i_send.at[0, l], i_recv.at[0, l], {"rows": mate},
            )
        return remote(
            prev_ref.at[rows, there], pv.at[x * blocks + l], i_send.at[1, l], i_recv.at[1, l], {"rows": mate}
        )

    def arrived_tile(src, l):
        dst = ext[0].at[blocks + y * blocks + l] if src == 0 else pv.at[y * blocks + l]
        return remote(dst, dst, i_send.at[src, l], i_recv.at[src, l], {"rows": mate})

    places = remote(vmine, vpair, w_send.at[0], w_recv.at[me], {"rows": mate})
    places_in = remote(vmine, vpair, w_send.at[0], w_recv.at[mate], {"rows": mate})

    def tiles(k, l):
        by_far = l < 3
        src = {
            0: ham.at[l], 1: ham.at[l], 2: hb.at[1, l], 3: ham.at[l], 4: hb.at[3, l],
            5: hb.at[3, l] if by_far else hb.at[1, l], 6: hb.at[5, l],
        }[k]
        device = {
            0: {"cols": sib}, 1: {"cols": far}, 2: {"cols": sib}, 3: {"rows": mate}, 4: {"cols": sib},
            5: {"cols": far} if by_far else {"rows": mate}, 6: {"cols": sib},
        }[k]
        return remote(src, hb.at[k, l], h_send.at[k, l], h_recv.at[k, l], device)

    places.start()
    for l in range(blocks):
        start_tile(0, l).start()
    for l in range(blocks):
        tiles(3, l).start()
        tiles(1, l).start()
    for l in range(blocks):
        start_tile(1, l).start()
    for l in range(blocks):
        tiles(0, l).start()

    def halo(t, up):
        if up:
            src, dst, device = 2 * blocks, 0, me + 2
        else:
            src, dst, device = blocks, 3 * blocks, me - 2
        return remote(
            ext[t].at[pl.ds(src, blocks)], ext[t].at[pl.ds(dst, blocks)],
            t_send.at[t, int(up)], t_recv.at[t, int(up)], {"rows": device},
        )

    has_up = me + 2 < n
    has_down = me >= 2

    def send_halo(t, block):
        @pl.when((block == 0) & has_down)
        def _():
            halo(t, False).start()

        @pl.when((block == 1) & has_up)
        def _():
            halo(t, True).start()

    def recv_halo(t):
        @pl.when(has_down)
        def _():
            halo(t, True).wait_recv()

        @pl.when(has_up)
        def _():
            halo(t, False).wait_recv()

    def drain_halo(t):
        @pl.when(has_up)
        def _():
            halo(t, True).wait_send()

        @pl.when(has_down)
        def _():
            halo(t, False).wait_send()

    for c in local[2::2]:
        c.wait()
    send_halo(0, x)

    npairs = pairs.shape[0]
    natoms = sizes.shape[1]
    atom = lax.broadcasted_iota(jnp.int32, (npairs, natoms), 1)
    size_f = jnp.broadcast_to(sizes[...].astype(jnp.float32), (npairs, natoms))
    first = jnp.broadcast_to(pairs[:, 0:1], (npairs, natoms))
    second = jnp.broadcast_to(pairs[:, 1:2], (npairs, natoms))
    start = jnp.sum(jnp.where(atom < first, size_f, 0.0), axis=1, keepdims=True)
    count_a = jnp.sum(jnp.where(atom == first, size_f, 0.0), axis=1, keepdims=True)
    count_b = jnp.sum(jnp.where(atom == second, size_f, 0.0), axis=1, keepdims=True)
    all_cols = npairs * MAXF
    column = lax.broadcasted_iota(jnp.int32, (npairs, all_cols), 1)
    pair_id = lax.broadcasted_iota(jnp.int32, (npairs, all_cols), 0)
    inner = column - pair_id * MAXF
    mine = (inner >= 0) & (inner < MAXF)
    kept = mine & (inner.astype(jnp.float32) < jnp.broadcast_to(count_b, (npairs, all_cols)))

    def spread(value, where):
        return jnp.sum(
            jnp.where(where, jnp.broadcast_to(value, (npairs, all_cols)), 0.0), axis=0, keepdims=True
        )

    low = spread(start, mine)
    bounds[0] = jnp.broadcast_to(low, (8, all_cols))
    bounds[1] = jnp.broadcast_to(low + spread(count_a, kept), (8, all_cols))
    part[...] = jnp.zeros_like(part)

    for l in range(blocks):
        arrived_tile(0, l).wait_recv()
    send_halo(0, y)
    places_in.wait_recv()
    to_smem = (
        pltpu.make_async_copy(vmine, smine, l_sem.at[2 + 2 * blocks]),
        pltpu.make_async_copy(vpair, spair, l_sem.at[3 + 2 * blocks]),
    )
    for c in to_smem:
        c.start()
    for l in range(blocks):
        tiles(3, l).wait_recv()
        if l < 3:
            tiles(5, l).start()
        tiles(4, l).start()
        tiles(1, l).wait_recv()
        if l >= 3:
            tiles(5, l).start()
        tiles(2, l).start()
    for c in to_smem:
        c.wait()
    for c in local[:2] + local[3::2]:
        c.wait()

    owners = (mc, sib, far, (sib + 2) % 4)

    def row(t, l, own):
        acc = jnp.zeros((tile, half), jnp.float32)
        spots = smine if own else spair
        for q, owner in enumerate(owners):
            for s in range(own_slots):
                if own:
                    h = hown[l, s] if q == 0 else hb[q - 1, l, s]
                else:
                    h = hb[3 + q, l, s]
                v = ext[t][spots[l, owner * own_slots + s]]
                acc += jnp.dot(h, v, preferred_element_type=jnp.float32)
        at = (x if own else y) * blocks + l
        before = pv[at] if t == 0 else ext[t - 1][blocks + at]
        nxt = (2.0 * acc - before.astype(jnp.float32)).astype(jnp.bfloat16)
        if t < STEPS - 1:
            ext[t + 1][blocks + at] = nxt
        elif not own:
            fin[l] = nxt
        if own:
            rows = pl.ds(pl.multiple_of(l * tile, tile), tile)
            dens[rows, here] = dens[rows, here] + coef[t] * nxt.astype(jnp.float32)

    def back(t):
        src = ext[t + 1].at[pl.ds(blocks + y * blocks, blocks)] if t < STEPS - 1 else fin
        return remote(src, ret[t], r_send.at[t], r_recv.at[t], {"rows": mate})

    def own_rows(t):
        def body(l, carry):
            row(t, l, True)
            return carry

        lax.fori_loop(0, blocks, body, 0)
        if t < STEPS - 1:
            send_halo(t + 1, x)

    def mate_rows(t):
        def body(l, carry):
            row(t, l, False)
            return carry

        lax.fori_loop(0, blocks, body, 0)
        if t < STEPS - 1:
            send_halo(t + 1, y)
        back(t).start()

    recv_halo(0)
    for k in (0, 2):
        for l in range(blocks):
            tiles(k, l).wait_recv()
    own_rows(0)
    for l in range(blocks):
        tiles(5, l).wait_recv()
        tiles(6, l).start()
    for l in range(blocks):
        arrived_tile(1, l).wait_recv()
    for k in (4, 6):
        for l in range(blocks):
            tiles(k, l).wait_recv()
    mate_rows(0)
    for t in range(1, STEPS):
        recv_halo(t)
        mate_rows(t)
        own_rows(t)

    def gather_sums(span):
        def body(l, carry):
            rows = pl.ds(pl.multiple_of(l * tile, tile), tile)
            value = dens[rows, span]
            r = lax.broadcasted_iota(jnp.int32, (tile, half), 0) + (me * blocks + l) * tile
            r = r.astype(jnp.float32)
            keep = (r >= bounds[0, 0:1, span]) & (r < bounds[1, 0:1, span])
            sq = jnp.where(keep, value * value, 0.0)
            part[:, span] += jnp.sum(sq.reshape(tile // 8, 8, half), axis=0)
            return carry

        lax.fori_loop(0, blocks, body, 0)

    def add_back(times):
        def body(l, carry):
            rows = pl.ds(pl.multiple_of(l * tile, tile), tile)
            value = dens[rows, there]
            for t in times:
                value = value + coef[t] * ret[t][l].astype(jnp.float32)
            dens[rows, there] = value
            return carry

        lax.fori_loop(0, blocks, body, 0)

    gather_sums(here)
    for t in range(STEPS - 1):
        back(t).wait_recv()
    add_back(range(STEPS - 1))
    back(STEPS - 1).wait_recv()
    add_back((STEPS - 1,))
    gather_sums(there)

    places.wait_send()

    def share(j):
        return remote(part, wbuf.at[me], w_send.at[j], w_recv.at[n + me], {"rows": (me + j) % n})

    def landed(j):
        source = (me + j) % n
        return remote(part, wbuf.at[source], w_send.at[j], w_recv.at[n + source], {"rows": source})

    def push(j, carry):
        share(j).start()
        return carry

    lax.fori_loop(1, n, push, 0)
    for l in range(blocks):
        for k in range(7):
            tiles(k, l).wait_send()
        for src in range(2):
            start_tile(src, l).wait_send()
    for t in range(STEPS):
        drain_halo(t)
        back(t).wait_send()

    def collect(j, total):
        landed(j).wait_recv()
        return total + wbuf[(me + j) % n]

    total = lax.fori_loop(1, n, collect, part[...])
    summed = jnp.broadcast_to(jnp.sum(total, axis=0, keepdims=True), (npairs, all_cols))
    wib[...] = jnp.sum(jnp.where(mine, summed, 0.0), axis=1, keepdims=True)

    def drain(j, carry):
        share(j).wait_send()
        return carry

    lax.fori_loop(1, n, drain, 0)


def on_device(n, ham, cols, count, prev, now, dens_prev, coef, sizes, pairs):
    blocks, own_slots, tile, _ = ham.shape
    rows, width = now.shape
    half = width // 2
    npairs = pairs.shape[0]
    vmem = pl.BlockSpec(memory_space=pltpu.VMEM)
    smem = pl.BlockSpec(memory_space=pltpu.SMEM)
    free = pl.BlockSpec(memory_space=pl.ANY)
    dma = pltpu.SemaphoreType.DMA
    bf16 = jnp.bfloat16
    dens, wib = pl.pallas_call(
        functools.partial(kernel, n),
        out_shape=(
            jax.ShapeDtypeStruct((rows, width), jnp.float32),
            jax.ShapeDtypeStruct((npairs, 1), jnp.float32),
        ),
        in_specs=[free, vmem, vmem, free, free, free, smem, vmem, vmem],
        out_specs=(vmem, vmem),
        scratch_shapes=[
            pltpu.VMEM((blocks, own_slots, tile, tile), bf16),
            pltpu.VMEM((7, blocks, own_slots, tile, tile), bf16),
            pltpu.VMEM((2 * blocks, tile, half), bf16),
            pltpu.VMEM((blocks, tile, half), bf16),
            pltpu.VMEM((8, 128), jnp.int32),
            pltpu.VMEM((8, 128), jnp.int32),
            pltpu.SMEM((8, 128), jnp.int32),
            pltpu.SMEM((8, 128), jnp.int32),
            pltpu.VMEM((8, width), jnp.float32),
            pltpu.VMEM((2, 8, width), jnp.float32),
            pltpu.VMEM((n, 8, width), jnp.float32),
            dma((7, blocks)),
            dma((7, blocks)),
            dma((STEPS, 2)),
            dma((STEPS, 2)),
            dma((2, blocks)),
            dma((2, blocks)),
            dma((STEPS,)),
            dma((STEPS,)),
            dma((n,)),
            dma((2 * n,)),
            dma((4 + 2 * blocks,)),
        ]
        + [pltpu.VMEM((4 * blocks + 1, tile, half), bf16)] * STEPS
        + [pltpu.VMEM((blocks, tile, half), bf16)] * STEPS,
        compiler_params=pltpu.CompilerParams(
            collective_id=0, has_side_effects=True, vmem_limit_bytes=56 << 20
        ),
    )(ham, cols, count.reshape(-1, 1), prev, now, dens_prev, coef, sizes.reshape(1, -1), pairs)
    return dens, wib.reshape(npairs)


def solution(mesh):
    return jax.shard_map(
        functools.partial(on_device, mesh.shape["rows"]),
        mesh=mesh,
        in_specs=(
            P("rows", "cols", None, None),
            P("rows", None),
            P("rows"),
            P("rows", "cols"),
            P("rows", "cols"),
            P("rows", "cols"),
            P(),
            P(),
            P("cols", None),
        ),
        out_specs=(P("rows", "cols"), P("cols")),
        check_vma=False,
    )
```

```python
import functools

import jax
import jax.numpy as jnp
from jax import lax
from jax.experimental import pallas as pl
from jax.experimental.pallas import tpu as pltpu
from jax.sharding import PartitionSpec as P

MAXF = 16
STEPS = 3
MESH = pl.DeviceIdType.MESH


def kernel(
    n,
    ham,
    cols_ref,
    count_ref,
    prev_ref,
    now_ref,
    dens_in,
    coef,
    sizes,
    pairs,
    dens,
    wib,
    hown,
    hb,
    pv,
    fin,
    vmine,
    vpair,
    smine,
    spair,
    part,
    bounds,
    wbuf,
    h_send,
    h_recv,
    t_send,
    t_recv,
    i_send,
    i_recv,
    r_send,
    r_recv,
    w_send,
    w_recv,
    l_sem,
    *bufs,
):
    ext, ret = bufs[:STEPS], bufs[STEPS:]
    me = lax.axis_index("rows")
    mc = lax.axis_index("cols")
    x = me % 2
    y = 1 - x
    mate = me + 1 - 2 * x
    blocks, own_slots, tile, _ = ham.shape
    half = now_ref.shape[1] // 2
    zero_tile = 4 * blocks
    sib = mc + 1 - 2 * (mc % 2)
    far = (mc + 2) % 4
    here = pl.ds(pl.multiple_of(x * half, half), half)
    there = pl.ds(pl.multiple_of(y * half, half), half)

    def remote(src, dst, send, recv, device):
        return pltpu.make_async_remote_copy(
            src_ref=src, dst_ref=dst, send_sem=send, recv_sem=recv, device_id=device, device_id_type=MESH
        )

    local = [pltpu.make_async_copy(ham, hown, l_sem.at[0]), pltpu.make_async_copy(dens_in, dens, l_sem.at[1])]
    for l in range(blocks):
        rows = pl.ds(l * tile, tile)
        local.append(
            pltpu.make_async_copy(now_ref.at[rows, here], ext[0].at[blocks + x * blocks + l], l_sem.at[2 + 2 * l])
        )
        local.append(pltpu.make_async_copy(prev_ref.at[rows, here], pv.at[x * blocks + l], l_sem.at[3 + 2 * l]))
    for c in local[2:] + local[:2]:
        c.start()

    barrier = pltpu.get_barrier_semaphore()

    def greet(j, carry):
        pl.semaphore_signal(barrier, inc=1, device_id={"rows": (me + j) % n}, device_id_type=MESH)
        return carry

    lax.fori_loop(1, n, greet, 0)
    pl.semaphore_signal(barrier, inc=1, device_id={"cols": sib}, device_id_type=MESH)
    pl.semaphore_signal(barrier, inc=1, device_id={"cols": far}, device_id_type=MESH)

    first_tile = (me - x) * blocks
    nslots = cols_ref.shape[1]
    tc = cols_ref[...]
    slot_id = lax.broadcasted_iota(jnp.int32, (blocks, nslots), 1)
    live = (slot_id < jnp.broadcast_to(count_ref[...], (blocks, nslots))) & (tc >= 0) & (tc < blocks * n)
    place = jnp.where(live, jnp.clip(tc - first_tile + blocks, 0, zero_tile - 1), zero_tile)
    vmine[...] = jnp.full(vmine.shape, zero_tile, jnp.int32)
    vmine[0:blocks, 0:nslots] = place
    for t in range(STEPS):
        ext[t][zero_tile] = jnp.zeros((tile, half), jnp.bfloat16)
    pl.semaphore_wait(barrier, n + 1)

    def start_tile(src, l):
        rows = pl.ds(l * tile, tile)
        if src == 0:
            return remote(
                now_ref.at[rows, there], ext[0].at[blocks + x * blocks + l],
                i_send.at[0, l], i_recv.at[0, l], {"rows": mate},
            )
        return remote(
            prev_ref.at[rows, there], pv.at[x * blocks + l], i_send.at[1, l], i_recv.at[1, l], {"rows": mate}
        )

    def arrived_tile(src, l):
        dst = ext[0].at[blocks + y * blocks + l] if src == 0 else pv.at[y * blocks + l]
        return remote(dst, dst, i_send.at[src, l], i_recv.at[src, l], {"rows": mate})

    places = remote(vmine, vpair, w_send.at[0], w_recv.at[me], {"rows": mate})
    places_in = remote(vmine, vpair, w_send.at[0], w_recv.at[mate], {"rows": mate})

    def tiles(k, l):
        by_far = l < 3
        src = {
            0: ham.at[l], 1: ham.at[l], 2: hb.at[1, l], 3: ham.at[l], 4: hb.at[3, l],
            5: hb.at[3, l] if by_far else hb.at[1, l], 6: hb.at[5, l],
        }[k]
        device = {
            0: {"cols": sib}, 1: {"cols": far}, 2: {"cols": sib}, 3: {"rows": mate}, 4: {"cols": sib},
            5: {"cols": far} if by_far else {"rows": mate}, 6: {"cols": sib},
        }[k]
        return remote(src, hb.at[k, l], h_send.at[k, l], h_recv.at[k, l], device)

    places.start()
    for l in range(blocks):
        start_tile(0, l).start()
    for l in range(blocks):
        tiles(3, l).start()
        tiles(1, l).start()
    for l in range(blocks):
        start_tile(1, l).start()
    for l in range(blocks):
        tiles(0, l).start()

    def halo(t, up, l):
        if up:
            src, dst, device = 2 * blocks, 0, me + 2
        else:
            src, dst, device = blocks, 3 * blocks, me - 2
        return remote(
            ext[t].at[src + l], ext[t].at[dst + l],
            t_send.at[t, int(up), l], t_recv.at[t, int(up), l], {"rows": device},
        )

    has_up = me + 2 < n
    has_down = me >= 2

    def send_halo(t, block, l):
        @pl.when((block == 0) & has_down)
        def _():
            halo(t, False, l).start()

        @pl.when((block == 1) & has_up)
        def _():
            halo(t, True, l).start()

    def recv_halo(t):
        @pl.when(has_down)
        def _():
            for l in range(blocks):
                halo(t, True, l).wait_recv()

        @pl.when(has_up)
        def _():
            for l in range(blocks):
                halo(t, False, l).wait_recv()

    def drain_halo(t):
        @pl.when(has_up)
        def _():
            for l in range(blocks):
                halo(t, True, l).wait_send()

        @pl.when(has_down)
        def _():
            for l in range(blocks):
                halo(t, False, l).wait_send()

    for c in local[2::2]:
        c.wait()
    for l in range(blocks):
        send_halo(0, x, l)

    npairs = pairs.shape[0]
    natoms = sizes.shape[1]
    atom = lax.broadcasted_iota(jnp.int32, (npairs, natoms), 1)
    size_f = jnp.broadcast_to(sizes[...].astype(jnp.float32), (npairs, natoms))
    first = jnp.broadcast_to(pairs[:, 0:1], (npairs, natoms))
    second = jnp.broadcast_to(pairs[:, 1:2], (npairs, natoms))
    start = jnp.sum(jnp.where(atom < first, size_f, 0.0), axis=1, keepdims=True)
    count_a = jnp.sum(jnp.where(atom == first, size_f, 0.0), axis=1, keepdims=True)
    count_b = jnp.sum(jnp.where(atom == second, size_f, 0.0), axis=1, keepdims=True)
    all_cols = npairs * MAXF
    column = lax.broadcasted_iota(jnp.int32, (npairs, all_cols), 1)
    pair_id = lax.broadcasted_iota(jnp.int32, (npairs, all_cols), 0)
    inner = column - pair_id * MAXF
    mine = (inner >= 0) & (inner < MAXF)
    kept = mine & (inner.astype(jnp.float32) < jnp.broadcast_to(count_b, (npairs, all_cols)))

    def spread(value, where):
        return jnp.sum(
            jnp.where(where, jnp.broadcast_to(value, (npairs, all_cols)), 0.0), axis=0, keepdims=True
        )

    low = spread(start, mine)
    bounds[0] = jnp.broadcast_to(low, (8, all_cols))
    bounds[1] = jnp.broadcast_to(low + spread(count_a, kept), (8, all_cols))
    part[...] = jnp.zeros_like(part)

    for l in range(blocks):
        arrived_tile(0, l).wait_recv()
        send_halo(0, y, l)
    places_in.wait_recv()
    to_smem = (
        pltpu.make_async_copy(vmine, smine, l_sem.at[2 + 2 * blocks]),
        pltpu.make_async_copy(vpair, spair, l_sem.at[3 + 2 * blocks]),
    )
    for c in to_smem:
        c.start()
    for l in range(blocks):
        tiles(3, l).wait_recv()
        if l < 3:
            tiles(5, l).start()
        tiles(4, l).start()
        tiles(1, l).wait_recv()
        if l >= 3:
            tiles(5, l).start()
        tiles(2, l).start()
    for c in to_smem:
        c.wait()
    for c in local[:2] + local[3::2]:
        c.wait()

    owners = (mc, sib, far, (sib + 2) % 4)

    def row(t, l, own):
        acc = jnp.zeros((tile, half), jnp.float32)
        spots = smine if own else spair
        for q, owner in enumerate(owners):
            for s in range(own_slots):
                if own:
                    h = hown[l, s] if q == 0 else hb[q - 1, l, s]
                else:
                    h = hb[3 + q, l, s]
                v = ext[t][spots[l, owner * own_slots + s]]
                acc += jnp.dot(h, v, preferred_element_type=jnp.float32)
        at = (x if own else y) * blocks + l
        before = pv[at] if t == 0 else ext[t - 1][blocks + at]
        nxt = (2.0 * acc - before.astype(jnp.float32)).astype(jnp.bfloat16)
        if t < STEPS - 1:
            ext[t + 1][blocks + at] = nxt
        elif not own:
            fin[l] = nxt
        if own:
            rows = pl.ds(pl.multiple_of(l * tile, tile), tile)
            dens[rows, here] = dens[rows, here] + coef[t] * nxt.astype(jnp.float32)

    def back(t, l):
        src = ext[t + 1].at[blocks + y * blocks + l] if t < STEPS - 1 else fin.at[l]
        return remote(src, ret[t].at[l], r_send.at[t, l], r_recv.at[t, l], {"rows": mate})

    def own_rows(t):
        def body(l, carry):
            row(t, l, True)
            if t < STEPS - 1:
                send_halo(t + 1, x, l)
            return carry

        lax.fori_loop(0, blocks, body, 0)

    def mate_row(t, l):
        row(t, l, False)
        if t < STEPS - 1:
            send_halo(t + 1, y, l)
        back(t, l).start()

    def mate_rows(t):
        def body(l, carry):
            mate_row(t, l)
            return carry

        lax.fori_loop(0, blocks, body, 0)

    recv_halo(0)
    for k in (0, 2):
        for l in range(blocks):
            tiles(k, l).wait_recv()
    own_rows(0)
    for l in range(blocks + 1):
        if l < blocks:
            tiles(5, l).wait_recv()
            tiles(6, l).start()
        if l > 0:
            arrived_tile(1, l - 1).wait_recv()
            tiles(4, l - 1).wait_recv()
            tiles(6, l - 1).wait_recv()
            mate_row(0, l - 1)
    for t in range(1, STEPS):
        recv_halo(t)
        mate_rows(t)
        own_rows(t)

    def gather_sums(span):
        def body(l, carry):
            rows = pl.ds(pl.multiple_of(l * tile, tile), tile)
            value = dens[rows, span]
            r = lax.broadcasted_iota(jnp.int32, (tile, half), 0) + (me * blocks + l) * tile
            r = r.astype(jnp.float32)
            keep = (r >= bounds[0, 0:1, span]) & (r < bounds[1, 0:1, span])
            sq = jnp.where(keep, value * value, 0.0)
            part[:, span] += jnp.sum(sq.reshape(tile // 8, 8, half), axis=0)
            return carry

        lax.fori_loop(0, blocks, body, 0)

    def add_back(times):
        def body(l, carry):
            rows = pl.ds(pl.multiple_of(l * tile, tile), tile)
            value = dens[rows, there]
            for t in times:
                value = value + coef[t] * ret[t][l].astype(jnp.float32)
            dens[rows, there] = value
            return carry

        lax.fori_loop(0, blocks, body, 0)

    gather_sums(here)
    for t in range(STEPS - 1):
        for l in range(blocks):
            back(t, l).wait_recv()
    add_back(range(STEPS - 1))
    for l in range(blocks):
        back(STEPS - 1, l).wait_recv()
    add_back((STEPS - 1,))
    gather_sums(there)

    places.wait_send()

    def share(j):
        return remote(part, wbuf.at[me], w_send.at[j], w_recv.at[n + me], {"rows": (me + j) % n})

    def landed(j):
        source = (me + j) % n
        return remote(part, wbuf.at[source], w_send.at[j], w_recv.at[n + source], {"rows": source})

    def push(j, carry):
        share(j).start()
        return carry

    lax.fori_loop(1, n, push, 0)
    for l in range(blocks):
        for k in range(7):
            tiles(k, l).wait_send()
        for src in range(2):
            start_tile(src, l).wait_send()
    for t in range(STEPS):
        drain_halo(t)
        for l in range(blocks):
            back(t, l).wait_send()

    def collect(j, total):
        landed(j).wait_recv()
        return total + wbuf[(me + j) % n]

    total = lax.fori_loop(1, n, collect, part[...])
    summed = jnp.broadcast_to(jnp.sum(total, axis=0, keepdims=True), (npairs, all_cols))
    wib[...] = jnp.sum(jnp.where(mine, summed, 0.0), axis=1, keepdims=True)

    def drain(j, carry):
        share(j).wait_send()
        return carry

    lax.fori_loop(1, n, drain, 0)


def on_device(n, ham, cols, count, prev, now, dens_prev, coef, sizes, pairs):
    blocks, own_slots, tile, _ = ham.shape
    rows, width = now.shape
    half = width // 2
    npairs = pairs.shape[0]
    vmem = pl.BlockSpec(memory_space=pltpu.VMEM)
    smem = pl.BlockSpec(memory_space=pltpu.SMEM)
    free = pl.BlockSpec(memory_space=pl.ANY)
    dma = pltpu.SemaphoreType.DMA
    bf16 = jnp.bfloat16
    dens, wib = pl.pallas_call(
        functools.partial(kernel, n),
        out_shape=(
            jax.ShapeDtypeStruct((rows, width), jnp.float32),
            jax.ShapeDtypeStruct((npairs, 1), jnp.float32),
        ),
        in_specs=[free, vmem, vmem, free, free, free, smem, vmem, vmem],
        out_specs=(vmem, vmem),
        scratch_shapes=[
            pltpu.VMEM((blocks, own_slots, tile, tile), bf16),
            pltpu.VMEM((7, blocks, own_slots, tile, tile), bf16),
            pltpu.VMEM((2 * blocks, tile, half), bf16),
            pltpu.VMEM((blocks, tile, half), bf16),
            pltpu.VMEM((8, 128), jnp.int32),
            pltpu.VMEM((8, 128), jnp.int32),
            pltpu.SMEM((8, 128), jnp.int32),
            pltpu.SMEM((8, 128), jnp.int32),
            pltpu.VMEM((8, width), jnp.float32),
            pltpu.VMEM((2, 8, width), jnp.float32),
            pltpu.VMEM((n, 8, width), jnp.float32),
            dma((7, blocks)),
            dma((7, blocks)),
            dma((STEPS, 2, blocks)),
            dma((STEPS, 2, blocks)),
            dma((2, blocks)),
            dma((2, blocks)),
            dma((STEPS, blocks)),
            dma((STEPS, blocks)),
            dma((n,)),
            dma((2 * n,)),
            dma((4 + 2 * blocks,)),
        ]
        + [pltpu.VMEM((4 * blocks + 1, tile, half), bf16)] * STEPS
        + [pltpu.VMEM((blocks, tile, half), bf16)] * STEPS,
        compiler_params=pltpu.CompilerParams(
            collective_id=0, has_side_effects=True, vmem_limit_bytes=56 << 20
        ),
    )(ham, cols, count.reshape(-1, 1), prev, now, dens_prev, coef, sizes.reshape(1, -1), pairs)
    return dens, wib.reshape(npairs)


def solution(mesh):
    return jax.shard_map(
        functools.partial(on_device, mesh.shape["rows"]),
        mesh=mesh,
        in_specs=(
            P("rows", "cols", None, None),
            P("rows", None),
            P("rows"),
            P("rows", "cols"),
            P("rows", "cols"),
            P("rows", "cols"),
            P(),
            P(),
            P("cols", None),
        ),
        out_specs=(P("rows", "cols"), P("cols")),
        check_vma=False,
    )
```
